256 devices in a mesh: dp: 8 (over y, core), expert: 32 (over x, z).
Axes of the slice: x: 4, y: 4, z: 8, core: 2. Of those that a mesh axis runs over, the one named last changes fastest.
Arguments:
- dense_partials: float32 [8, 1024, 4096], P('dp', None, 'expert'), may hold values from -6 to 6
- dense_param: float32 [1024, 4096], P('dp', 'expert'), may hold values from -3 to 3
- dense_m: float32 [1024, 4096], P('dp', 'expert'), may hold values from -18 to 18
- dense_v: float32 [1024, 4096], P('dp', 'expert'), may hold values from 1 to 10
- sent_inputs: bfloat16 [1024, 128, 2048], P('expert', None, 'dp'), may hold values from -6 to 6
- sent_outputs: bfloat16 [1024, 128, 1408], P('expert'), may hold values from -0.23925781 to 0.23925781
- counts: int32 [32, 32], replicated, may hold values from 0 to 128, as said below
- expert_param: float32 [32, 2048, 1408], P('expert', 'dp'), may hold values from -3 to 3
- expert_m: float32 [32, 2048, 1408], P('expert', 'dp'), may hold values from -18 to 18
- expert_v: float32 [32, 2048, 1408], P('expert', 'dp'), may hold values from 1 to 10
Outputs:
- dense_param_new: float32 [1024, 4096], P('dp', 'expert')
- dense_m_new: float32 [1024, 4096], P('dp', 'expert')
- dense_v_new: float32 [1024, 4096], P('dp', 'expert')
- expert_param_new: float32 [32, 2048, 1408], P('expert', 'dp')
- expert_m_new: float32 [32, 2048, 1408], P('expert', 'dp')
- expert_v_new: float32 [32, 2048, 1408], P('expert', 'dp')
The draws below stay inside these ranges and needn't reach their ends.
Inputs may be any that keep to these rules, and one draw needn't show every extreme that they name: counts[j, e] is the number of live leading slots of block j * 32 + e; in every draw some expert receives 128 live slots from every token group.
All inputs are finite; a program needn't handle non-finite values.
Results may differ from the reference program's by a relative error of at most 0.0003.
Values may be sent and summed in bfloat16 or wider, within the bound.
A program may use at most 128 MiB of HBM per device.

```python
import math
import jax
import jax.numpy as jnp
from jax import lax

D = 4096
FF = 1408
D_WIN = 2048
CAP = 128
EXPERTS = 32
DENSE_ROWS = 1024
N_DP = 8
N_EXPERT = 32


def draw_counts(key, part):
    key = jax.random.fold_in(key, 5)
    key_base, key_level, key_full = jax.random.split(key, 3)
    base = jax.random.randint(key_base, (N_EXPERT, EXPERTS), 0, CAP + 1)
    level = jax.random.randint(key_level, (1, EXPERTS), 1, 5)
    filled = jnp.minimum(CAP, base * level // 2)
    full = jax.random.randint(key_full, (), 0, EXPERTS)
    column = lax.broadcasted_iota(jnp.int32, (N_EXPERT, EXPERTS), 1)
    return jnp.where(column == full, CAP, filled).astype(jnp.int32)


def levels(stream_key, extent, cuts, smallest, high):
    def one(position, shards_of):
        draws = jax.random.uniform(jax.random.fold_in(jax.random.fold_in(stream_key, 6), position), (shards_of,), jnp.float32, smallest / len(cuts), high / len(cuts))
        return jnp.repeat(jnp.exp(draws), extent[position] // shards_of).reshape((-1,) + (1,) * (len(extent) - position - 1))

    loudness = one(*cuts[0])
    for cut in cuts[1:]:
        loudness = loudness * one(*cut)
    return loudness


def bell_draw(rng, extent, spread, reach, cuts=(), dtype=jnp.bfloat16):
    entries = spread * jax.random.normal(rng, extent, jnp.float32)
    if cuts:
        entries = entries * levels(rng, extent, cuts, -0.22, 0.18)
    return jnp.clip(entries, -reach, reach).astype(dtype)


def setup_inputs(seed: int = 0) -> dict:
    arg_keys = jax.random.split(jax.random.key(seed), 11)
    return {
        "dense_partials": bell_draw(arg_keys[0], (N_DP, DENSE_ROWS, D), 1.0, 6.0, ((0, 8), (2, 32)), jnp.float32),
        "dense_param": bell_draw(arg_keys[1], (DENSE_ROWS, D), 0.5, 3.0, ((0, 8), (1, 32)), jnp.float32),
        "dense_m": bell_draw(arg_keys[2], (DENSE_ROWS, D), 3.0, 18.0, ((0, 8), (1, 32)), jnp.float32),
        "dense_v": jnp.clip(jnp.exp(math.log(10.0) - 2.3025851 * jax.random.uniform(arg_keys[3], (DENSE_ROWS, D), jnp.float32) ** levels(arg_keys[3], (DENSE_ROWS, D), ((0, 8), (1, 32)), -0.2, 0.2)), 1.0, 10.0),
        "sent_inputs": bell_draw(arg_keys[4], (N_EXPERT * EXPERTS, CAP, D_WIN), 1.0, 6.0, ((0, 32), (2, 8))),
        "sent_outputs": bell_draw(arg_keys[5], (N_EXPERT * EXPERTS, CAP, FF), 0.04, 0.23925781, ((0, 32),)),
        "counts": draw_counts(jax.random.fold_in(arg_keys[10], 71), 0),
        "expert_param": bell_draw(arg_keys[7], (EXPERTS, D_WIN, FF), 0.5, 3.0, ((0, 32), (1, 8)), jnp.float32),
        "expert_m": bell_draw(arg_keys[8], (EXPERTS, D_WIN, FF), 3.0, 18.0, ((0, 32), (1, 8)), jnp.float32),
        "expert_v": jnp.clip(jnp.exp(math.log(10.0) - 2.3025851 * jax.random.uniform(arg_keys[9], (EXPERTS, D_WIN, FF), jnp.float32) ** levels(arg_keys[9], (EXPERTS, D_WIN, FF), ((0, 32), (1, 8)), -0.2, 0.2)), 1.0, 10.0),
    }


def adamw(param, moment, second, grad):
    moment_new = 0.9 * moment + 0.1 * grad
    second_new = 0.95 * second + 0.05 * grad * grad
    corrected = moment_new / (1.0 - 0.9 ** 10)
    scaled = jnp.sqrt(second_new / (1.0 - 0.95 ** 10)) + 1e-08
    param_new = param - 0.01 * (corrected / scaled + 0.1 * param)
    return (param_new, moment_new, second_new)

def reference(dense_partials, dense_param, dense_m, dense_v, sent_inputs, sent_outputs, counts, expert_param, expert_m, expert_v):
    dense_grad = lax.optimization_barrier(jnp.sum(dense_partials, axis=0))
    inputs_by = sent_inputs.reshape(N_EXPERT, EXPERTS, CAP, D_WIN).transpose(1, 0, 2, 3)
    outputs_by = sent_outputs.reshape(N_EXPERT, EXPERTS, CAP, FF).transpose(1, 0, 2, 3)
    counts_by = counts.T

    def one_expert(items):
        inputs, outputs, column = items
        live = lax.broadcasted_iota(jnp.int32, (N_EXPERT, CAP), 1) < column[:, None]
        masked = jnp.where(live[:, :, None], outputs, jnp.zeros_like(outputs))
        return jnp.dot(inputs.reshape(-1, D_WIN).T, masked.reshape(-1, FF), preferred_element_type=jnp.float32)
    expert_grad = lax.map(one_expert, (inputs_by, outputs_by, counts_by))
    dp_new, dm_new, dv_new = adamw(dense_param, dense_m, dense_v, dense_grad)
    ep_new, em_new, ev_new = adamw(expert_param, expert_m, expert_v, expert_grad)
    return (dp_new, dm_new, dv_new, ep_new, em_new, ev_new)
```

```python
import jax
import jax.numpy as jnp
from jax import lax
from jax.sharding import PartitionSpec as P


def adamw(param, moment, second, grad):
    moment_new = 0.9 * moment + 0.1 * grad
    second_new = 0.95 * second + 0.05 * grad * grad
    corrected = moment_new / (1.0 - 0.9**10)
    scaled = jnp.sqrt(second_new / (1.0 - 0.95**10)) + 1e-08
    param_new = param - 0.01 * (corrected / scaled + 0.1 * param)
    return (param_new, moment_new, second_new)


def per_device(
    dense_partials,
    dense_param,
    dense_m,
    dense_v,
    sent_inputs,
    sent_outputs,
    counts,
    expert_param,
    expert_m,
    expert_v,
):
    summed = lax.psum_scatter(dense_partials, "dp", scatter_dimension=1, tiled=True)
    dense_grad = summed[0]
    replicas = lax.axis_size("dp")
    blocks, slots, width_out = sent_outputs.shape
    width_in = sent_inputs.shape[2]
    part = slots // replicas
    share = lax.dynamic_slice_in_dim(sent_outputs, lax.axis_index("dp") * part, part, 1)
    arrived_share = lax.all_to_all(share, "expert", split_axis=0, concat_axis=0, tiled=True)
    arrived_in = lax.all_to_all(sent_inputs, "expert", split_axis=0, concat_axis=0, tiled=True)
    arrived_out = lax.all_gather(arrived_share, "dp")
    column = lax.dynamic_slice_in_dim(counts, lax.axis_index("expert"), 1, 1)
    live = lax.broadcasted_iota(jnp.int32, (blocks, slots), 1) < column
    masked = jnp.where(live[:, :, None], arrived_in, jnp.zeros_like(arrived_in))
    expert_grad = lax.dot_general(
        masked.reshape(blocks, replicas, part, width_in).transpose(1, 0, 2, 3).reshape(blocks * slots, width_in),
        arrived_out.reshape(blocks * slots, width_out),
        (((0,), (0,)), ((), ())),
        preferred_element_type=jnp.float32,
    )
    dp_new, dm_new, dv_new = adamw(dense_param, dense_m, dense_v, dense_grad)
    ep_new, em_new, ev_new = adamw(expert_param, expert_m, expert_v, expert_grad[None])
    return (dp_new, dm_new, dv_new, ep_new, em_new, ev_new)


def solution(mesh):
    in_specs = (
        P("dp", None, "expert"),
        P("dp", "expert"),
        P("dp", "expert"),
        P("dp", "expert"),
        P("expert", None, "dp"),
        P("expert", None, None),
        P(),
        P("expert", "dp", None),
        P("expert", "dp", None),
        P("expert", "dp", None),
    )
    out_specs = (
        P("dp", "expert"),
        P("dp", "expert"),
        P("dp", "expert"),
        P("expert", "dp", None),
        P("expert", "dp", None),
        P("expert", "dp", None),
    )
    return jax.shard_map(
        per_device, mesh=mesh, in_specs=in_specs, out_specs=out_specs, check_vma=False
    )
```

```python
import jax
import jax.numpy as jnp
from jax import lax
from jax.experimental import pallas as pl
from jax.experimental.pallas import tpu as pltpu
from jax.sharding import PartitionSpec as P

MESH = pl.DeviceIdType.MESH
X, Z, Y = 4, 8, 4
DP = 2 * Y
BF16_ROWS = 16


def adamw(param, moment, second, grad):
    moment_new = 0.9 * moment + 0.1 * grad
    second_new = 0.95 * second + 0.05 * grad * grad
    corrected = moment_new / (1.0 - 0.9**10)
    scaled = jnp.sqrt(second_new / (1.0 - 0.95**10)) + 1e-08
    param_new = param - 0.01 * (corrected / scaled + 0.1 * param)
    return (param_new, moment_new, second_new)


def wave(k):
    half = (k + 1) // 2
    return 4 + half if k % 2 == 0 else 4 - half


def exchange(
    counts,
    partials,
    inputs,
    outputs,
    grad,
    dense,
    ins,
    outs,
    rows,
    out_send,
    out_recv,
    in_send,
    in_recv,
    row_send,
    row_recv,
    y_send,
    y_recv,
    core_send,
    core_recv,
):
    d, e = lax.axis_index("dp"), lax.axis_index("expert")
    y, c = d // 2, d % 2
    x, z = e // Z, e % Z
    ahead = lax.rem(y + 1 + 2 * c, Y)
    behind = lax.rem(y + 3 - 2 * c, Y)
    across = lax.rem(y + 2, Y)
    sibling = 2 * y + 1 - c

    def remote(src, dst, send, recv, dp, expert):
        return pltpu.make_async_remote_copy(
            src_ref=src,
            dst_ref=dst,
            send_sem=send,
            recv_sem=recv,
            device_id=(dp, expert),
            device_id_type=MESH,
        )

    def peer(dx, dz):
        return lax.rem(x + dx, X) * Z + lax.rem(z + dz, Z)

    barrier = pltpu.get_barrier_semaphore()
    for dx in range(X):
        for dz in range(Z):
            if dx or dz:
                pl.semaphore_signal(barrier, inc=1, device_id=(d, peer(dx, dz)), device_id_type=MESH)
    for step in range(1, DP):
        pl.semaphore_signal(barrier, inc=1, device_id=(lax.rem(d + step, DP), e), device_id_type=MESH)
    pl.semaphore_wait(barrier, X * Z - 1 + DP - 1)

    def send_wave(k, src_of, buffer, send, recv):
        dz = wave(k)
        slot = z * X + x
        for dx in (2, 1, 3, 0):
            there = peer(dx, dz)
            if dx or dz:
                remote(src_of(there), buffer(slot), send, recv.at[z], d, there).start()
            else:
                pltpu.make_async_copy(src_of(there), buffer(slot), recv.at[z]).start()

    def arrived(k):
        from_z = lax.rem(z + Z - wave(k), Z)
        return from_z, pl.ds(pl.multiple_of(from_z * X, X), X)

    def wait_recv(ref, recv):
        remote(ref, ref, recv, recv, d, e).wait_recv()

    def out_src(there):
        return outputs.at[there, d]

    def in_src(there):
        return inputs.at[there]

    for k in range(Z):
        send_wave(k, out_src, lambda slot: outs.at[d, slot], out_send, out_recv)
    for step in range(1, DP):
        there = lax.rem(d + step, DP)
        remote(partials.at[there], rows.at[d], row_send, row_recv, there, e).start()
    pltpu.make_async_copy(partials.at[d], rows.at[d], row_recv).start()

    def own(k):
        from_z, slots = arrived(k)
        piece = outs.at[d, slots]
        wait_recv(piece, out_recv.at[from_z])
        remote(piece, piece, y_send, y_recv.at[k, 0], 2 * ahead + c, e).start()
        remote(piece, piece, y_send, y_recv.at[k, 1], 2 * behind + c, e).start()
        remote(piece, piece, core_send, core_recv.at[k, 0], sibling, e).start()

    def near(k):
        _, slots = arrived(k)
        piece = outs.at[2 * behind + c, slots]
        wait_recv(piece, y_recv.at[k, 0])
        remote(piece, piece, y_send, y_recv.at[k, 2], 2 * ahead + c, e).start()
        remote(piece, piece, core_send, core_recv.at[k, 1], sibling, e).start()
        piece = outs.at[2 * ahead + c, slots]
        wait_recv(piece, y_recv.at[k, 1])
        remote(piece, piece, core_send, core_recv.at[k, 2], sibling, e).start()

    def far(k):
        _, slots = arrived(k)
        piece = outs.at[2 * across + c, slots]
        wait_recv(piece, y_recv.at[k, 2])
        remote(piece, piece, core_send, core_recv.at[k, 3], sibling, e).start()

    for k in range(Z + 2):
        if k < Z:
            own(k)
            send_wave(k, in_src, lambda slot: ins.at[:, slot], in_send, in_recv)
        if 1 <= k <= Z:
            near(k - 1)
        if k >= 2:
            far(k - 2)

    wait_recv(rows, row_recv)
    total = rows[0]
    for step in range(1, DP):
        total = total + rows[step]
    dense[...] = total

    for k in range(Z):
        from_z, slots = arrived(k)
        wait_recv(outs.at[sibling, slots], core_recv.at[k, 0])
        wait_recv(outs.at[2 * ahead + 1 - c, slots], core_recv.at[k, 1])
        wait_recv(outs.at[2 * behind + 1 - c, slots], core_recv.at[k, 2])
        wait_recv(outs.at[2 * across + 1 - c, slots], core_recv.at[k, 3])
        wait_recv(ins.at[:, slots], in_recv.at[from_z])
        live = []
        for from_x in range(X):
            block = ins[:, from_z * X + from_x]
            slot = BF16_ROWS * lax.broadcasted_iota(jnp.int32, block.shape, 0) + lax.broadcasted_iota(jnp.int32, block.shape, 1)
            live.append(jnp.where(slot < counts[from_x * Z + from_z, e], block, jnp.zeros_like(block)))
        left = jnp.stack(live, axis=1)
        right = outs[:, slots]
        product = lax.dot_general(
            left.reshape(-1, left.shape[-1]),
            right.reshape(-1, right.shape[-1]),
            (((0,), (0,)), ((), ())),
            preferred_element_type=jnp.float32,
        )
        if k == 0:
            grad[...] = product
        else:
            grad[...] += product

    def wait_send(ref, send):
        remote(ref, ref, send, send, d, e).wait_send()

    wait_send(outs.at[0, pl.ds(0, X * Z - 1)], out_send)
    wait_send(ins.at[:, pl.ds(0, X * Z - 1)], in_send)
    wait_send(rows.at[pl.ds(0, DP - 1)], row_send)
    wait_send(outs.at[pl.ds(0, 3)], y_send)
    wait_send(outs.at[pl.ds(0, 4)], core_send)


def per_device(
    dense_partials,
    dense_param,
    dense_m,
    dense_v,
    sent_inputs,
    sent_outputs,
    counts,
    expert_param,
    expert_m,
    expert_v,
):
    blocks, slots, width_in = sent_inputs.shape
    width_out = sent_outputs.shape[2]
    part = slots // DP
    dense_rows, dense_width = dense_partials.shape[1] // DP, dense_partials.shape[2]
    dma = pltpu.SemaphoreType.DMA
    expert_grad, dense_grad = pl.pallas_call(
        exchange,
        name="exchange",
        out_shape=(
            jax.ShapeDtypeStruct((width_in, width_out), jnp.float32),
            jax.ShapeDtypeStruct((dense_rows, dense_width), jnp.float32),
        ),
        in_specs=[pl.BlockSpec(memory_space=pltpu.SMEM)] + [pl.BlockSpec(memory_space=pl.ANY)] * 3,
        out_specs=(pl.BlockSpec(memory_space=pltpu.VMEM),) * 2,
        scratch_shapes=[
            pltpu.VMEM((DP, blocks, part, width_in), jnp.bfloat16),
            pltpu.VMEM((DP, blocks, part, width_out), jnp.bfloat16),
            pltpu.VMEM((DP, dense_rows, dense_width), jnp.float32),
            dma,
            dma((Z,)),
            dma,
            dma((Z,)),
            dma,
            dma,
            dma,
            dma((Z, 3)),
            dma,
            dma((Z, 4)),
        ],
        cost_estimate=pl.CostEstimate(
            flops=2 * blocks * slots * width_in * width_out,
            bytes_accessed=2 * blocks * slots * (width_in + width_out),
            transcendentals=0,
        ),
        compiler_params=pltpu.CompilerParams(collective_id=0, has_side_effects=True, vmem_limit_bytes=48 << 20),
    )(
        counts,
        dense_partials.reshape(DP, dense_rows, dense_width),
        sent_inputs.reshape(blocks, DP, part, width_in),
        sent_outputs.reshape(blocks, DP, part, width_out),
    )
    dp_new, dm_new, dv_new = adamw(dense_param, dense_m, dense_v, dense_grad)
    ep_new, em_new, ev_new = adamw(expert_param, expert_m, expert_v, expert_grad[None])
    return (dp_new, dm_new, dv_new, ep_new, em_new, ev_new)


def solution(mesh):
    in_specs = (
        P("dp", None, "expert"),
        P("dp", "expert"),
        P("dp", "expert"),
        P("dp", "expert"),
        P("expert", None, "dp"),
        P("expert", None, None),
        P(),
        P("expert", "dp", None),
        P("expert", "dp", None),
        P("expert", "dp", None),
    )
    out_specs = (
        P("dp", "expert"),
        P("dp", "expert"),
        P("dp", "expert"),
        P("expert", "dp", None),
        P("expert", "dp", None),
        P("expert", "dp", None),
    )
    return jax.shard_map(per_device, mesh=mesh, in_specs=in_specs, out_specs=out_specs, check_vma=False)
```

```python
import jax
import jax.numpy as jnp
from jax import lax
from jax.experimental import pallas as pl
from jax.experimental.pallas import tpu as pltpu
from jax.sharding import PartitionSpec as P

MESH = pl.DeviceIdType.MESH
X, Z, Y = 4, 8, 4
DP = 2 * Y
BF16_ROWS = 16


def adamw(param, moment, second, grad):
    moment_new = 0.9 * moment + 0.1 * grad
    second_new = 0.95 * second + 0.05 * grad * grad
    corrected = moment_new / (1.0 - 0.9**10)
    scaled = jnp.sqrt(second_new / (1.0 - 0.95**10)) + 1e-08
    param_new = param - 0.01 * (corrected / scaled + 0.1 * param)
    return (param_new, moment_new, second_new)


def wave(k):
    half = (k + 1) // 2
    return 4 + half if k % 2 == 0 else 4 - half


def exchange(
    counts_hbm,
    partials,
    inputs,
    outputs,
    grad,
    dense,
    counts,
    ins,
    outs,
    relay_ins,
    relay_outs,
    rows,
    counts_sem,
    send,
    x_out_recv,
    x_in_recv,
    out_recv,
    in_recv,
    row_recv,
    y_recv,
    core_recv,
):
    d, e = lax.axis_index("dp"), lax.axis_index("expert")
    y, c = d // 2, d % 2
    x, z = e // Z, e % Z
    ahead = lax.rem(y + 1 + 2 * c, Y)
    behind = lax.rem(y + 3 - 2 * c, Y)
    across = lax.rem(y + 2, Y)
    sibling = 2 * y + 1 - c
    to_x, to_z, to_y, to_core, to_rows = (send.at[i] for i in range(5))

    def remote(src, dst, send, recv, dp, expert):
        return pltpu.make_async_remote_copy(
            src_ref=src,
            dst_ref=dst,
            send_sem=send,
            recv_sem=recv,
            device_id=(dp, expert),
            device_id_type=MESH,
        )

    def peer(dx, dz):
        return lax.rem(x + dx, X) * Z + lax.rem(z + dz, Z)

    load_counts = pltpu.make_async_copy(counts_hbm, counts, counts_sem)
    load_counts.start()
    barrier = pltpu.get_barrier_semaphore()
    for dz in range(1, Z):
        pl.semaphore_signal(barrier, inc=1, device_id=(d, peer(0, dz)), device_id_type=MESH)
    for dx in range(1, X):
        pl.semaphore_signal(barrier, inc=1, device_id=(d, peer(dx, 0)), device_id_type=MESH)
    for step in range(1, DP):
        pl.semaphore_signal(barrier, inc=1, device_id=(lax.rem(d + step, DP), e), device_id_type=MESH)
    pl.semaphore_wait(barrier, Z - 1 + X - 1 + DP - 1)

    def slot_of(source_z, dx):
        return source_z * X + dx

    def slots_from(k):
        return pl.ds(pl.multiple_of(lax.rem(z + Z - wave(k), Z) * X, X), X)

    def wait_recv(ref, recv):
        remote(ref, ref, recv, recv, d, e).wait_recv()

    def to_columns(k, src_of, buffer, relay, x_recv, recv):
        for dx in (2, 1, 3):
            block = src_of(peer(dx, wave(k)))
            if wave(k):
                remote(block, relay.at[k, dx - 1], to_x, x_recv.at[k], d, peer(dx, 0)).start()
            else:
                remote(block, buffer(pl.ds(slot_of(z, dx), 1)).at[0], to_x, recv.at[k], d, peer(dx, 0)).start()

    def own_column(k, src_of, buffer, recv):
        there = peer(0, wave(k))
        mine = buffer(pl.ds(slot_of(z, 0), 1)).at[0]
        if wave(k):
            remote(src_of(there), mine, to_z, recv.at[k], d, there).start()
        else:
            pltpu.make_async_copy(src_of(there), mine, recv.at[k]).start()

    def relay_column(k, buffer, relay, x_recv, recv):
        if wave(k):
            wait_recv(relay.at[k], x_recv.at[k])
            remote(relay.at[k], buffer(pl.ds(slot_of(z, 1), X - 1)), to_z, recv.at[k], d, peer(0, wave(k))).start()

    def out_src(there):
        return outputs.at[there, d]

    def out_at(slots):
        return outs.at[d, slots]

    def in_src(there):
        return inputs.at[there]

    def in_at(slots):
        return ins.at[slots]

    for k in range(Z):
        own_column(k, out_src, out_at, out_recv)
        to_columns(k, out_src, out_at, relay_outs, x_out_recv, out_recv)
    for step in range(1, DP):
        there = lax.rem(d + step, DP)
        remote(partials.at[there], rows.at[d], to_rows, row_recv, there, e).start()
    pltpu.make_async_copy(partials.at[d], rows.at[d], row_recv).start()

    def own(k):
        piece = outs.at[d, slots_from(k)]
        wait_recv(piece, out_recv.at[k])
        remote(piece, piece, to_y, y_recv.at[k, 0], 2 * ahead + c, e).start()
        remote(piece, piece, to_y, y_recv.at[k, 1], 2 * behind + c, e).start()
        remote(piece, piece, to_core, core_recv.at[k, 0], sibling, e).start()

    def near(k):
        piece = outs.at[2 * behind + c, slots_from(k)]
        wait_recv(piece, y_recv.at[k, 0])
        remote(piece, piece, to_y, y_recv.at[k, 2], 2 * ahead + c, e).start()
        remote(piece, piece, to_core, core_recv.at[k, 1], sibling, e).start()
        piece = outs.at[2 * ahead + c, slots_from(k)]
        wait_recv(piece, y_recv.at[k, 1])
        remote(piece, piece, to_core, core_recv.at[k, 2], sibling, e).start()

    def far(k):
        piece = outs.at[2 * across + c, slots_from(k)]
        wait_recv(piece, y_recv.at[k, 2])
        remote(piece, piece, to_core, core_recv.at[k, 3], sibling, e).start()

    for i in range(Z + 5):
        if i < Z:
            relay_column(i, out_at, relay_outs, x_out_recv, out_recv)
            to_columns(i, in_src, in_at, relay_ins, x_in_recv, in_recv)
        if 3 <= i < Z + 3:
            own(i - 3)
        if 4 <= i < Z + 4:
            own_column(i - 4, in_src, in_at, in_recv)
            relay_column(i - 4, in_at, relay_ins, x_in_recv, in_recv)
            near(i - 4)
        if 5 <= i:
            far(i - 5)

    wait_recv(rows, row_recv)
    total = rows[0]
    for step in range(1, DP):
        total = total + rows[step]
    dense[...] = total
    load_counts.wait()

    for n, k in enumerate((0, 1, 2, 3, 4, 5, 7, 6)):
        slots = slots_from(k)
        wait_recv(outs.at[sibling, slots], core_recv.at[k, 0])
        wait_recv(outs.at[2 * ahead + 1 - c, slots], core_recv.at[k, 1])
        wait_recv(outs.at[2 * behind + 1 - c, slots], core_recv.at[k, 2])
        wait_recv(outs.at[2 * across + 1 - c, slots], core_recv.at[k, 3])
        wait_recv(ins.at[slots], in_recv.at[k])
        from_z = lax.rem(z + Z - wave(k), Z)
        live = []
        for dx in range(X):
            block = ins[slot_of(from_z, dx)]
            slot = BF16_ROWS * lax.broadcasted_iota(jnp.int32, block.shape, 0) + lax.broadcasted_iota(jnp.int32, block.shape, 1)
            count = counts[lax.rem(x + X - dx, X) * Z + from_z, e]
            live.append(jnp.where(slot < count, block, jnp.zeros_like(block)))
        left = jnp.stack(live, axis=1)
        right = outs[:, slots]
        product = lax.dot_general(
            left.reshape(-1, left.shape[-1]),
            right.reshape(-1, right.shape[-1]),
            (((0,), (0,)), ((), ())),
            preferred_element_type=jnp.float32,
        )
        if n == 0:
            grad[...] = product
        else:
            grad[...] += product

    def wait_send(ref, sem):
        remote(ref, ref, sem, sem, d, e).wait_send()

    wait_send(outs.at[0, pl.ds(0, Z * (X - 1))], to_x)
    wait_send(ins.at[pl.ds(0, Z * (X - 1))], to_x)
    wait_send(outs.at[0, pl.ds(0, (Z - 1) * X)], to_z)
    wait_send(ins.at[pl.ds(0, (Z - 1) * X)], to_z)
    wait_send(rows.at[pl.ds(0, DP - 1)], to_rows)
    wait_send(outs.at[pl.ds(0, 3)], to_y)
    wait_send(outs.at[pl.ds(0, 4)], to_core)


def per_device(
    dense_partials,
    dense_param,
    dense_m,
    dense_v,
    sent_inputs,
    sent_outputs,
    counts,
    expert_param,
    expert_m,
    expert_v,
):
    blocks, slots, width_in = sent_inputs.shape
    width_out = sent_outputs.shape[2]
    part = slots // DP
    dense_rows, dense_width = dense_partials.shape[1] // DP, dense_partials.shape[2]
    dma = pltpu.SemaphoreType.DMA
    expert_grad, dense_grad = pl.pallas_call(
        exchange,
        name="exchange",
        out_shape=(
            jax.ShapeDtypeStruct((width_in, width_out), jnp.float32),
            jax.ShapeDtypeStruct((dense_rows, dense_width), jnp.float32),
        ),
        in_specs=[pl.BlockSpec(memory_space=pltpu.HBM)] * 4,
        out_specs=(pl.BlockSpec(memory_space=pltpu.VMEM),) * 2,
        scratch_shapes=[
            pltpu.SMEM(counts.shape, counts.dtype),
            pltpu.VMEM((blocks, DP, part, width_in), jnp.bfloat16),
            pltpu.VMEM((DP, blocks, part, width_out), jnp.bfloat16),
            pltpu.VMEM((Z - 1, X - 1, DP, part, width_in), jnp.bfloat16),
            pltpu.VMEM((Z - 1, X - 1, part, width_out), jnp.bfloat16),
            pltpu.VMEM((DP, dense_rows, dense_width), jnp.float32),
            dma,
            dma((5,)),
            dma((Z - 1,)),
            dma((Z - 1,)),
            dma((Z,)),
            dma((Z,)),
            dma,
            dma((Z, 3)),
            dma((Z, 4)),
        ],
        cost_estimate=pl.CostEstimate(
            flops=2 * blocks * slots * width_in * width_out,
            bytes_accessed=2 * blocks * slots * (width_in + width_out),
            transcendentals=0,
        ),
        compiler_params=pltpu.CompilerParams(collective_id=0, has_side_effects=True, vmem_limit_bytes=48 << 20),
    )(
        counts,
        dense_partials.reshape(DP, dense_rows, dense_width),
        sent_inputs.reshape(blocks, DP, part, width_in),
        sent_outputs.reshape(blocks, DP, part, width_out),
    )
    dp_new, dm_new, dv_new = adamw(dense_param, dense_m, dense_v, dense_grad)
    ep_new, em_new, ev_new = adamw(expert_param, expert_m, expert_v, expert_grad[None])
    return (dp_new, dm_new, dv_new, ep_new, em_new, ev_new)


def solution(mesh):
    in_specs = (
        P("dp", None, "expert"),
        P("dp", "expert"),
        P("dp", "expert"),
        P("dp", "expert"),
        P("expert", None, "dp"),
        P("expert", None, None),
        P(),
        P("expert", "dp", None),
        P("expert", "dp", None),
        P("expert", "dp", None),
    )
    out_specs = (
        P("dp", "expert"),
        P("dp", "expert"),
        P("dp", "expert"),
        P("expert", "dp", None),
        P("expert", "dp", None),
        P("expert", "dp", None),
    )
    return jax.shard_map(per_device, mesh=mesh, in_specs=in_specs, out_specs=out_specs, check_vma=False)
```

```python
import jax
import jax.numpy as jnp
from jax import lax
from jax.experimental import pallas as pl
from jax.experimental.pallas import tpu as pltpu
from jax.sharding import PartitionSpec as P

MESH = pl.DeviceIdType.MESH
X, Z, Y = 4, 8, 4
DP = 2 * Y
BF16_ROWS = 16
STRETCHES = 8


def adamw(param, moment, second, grad):
    moment_new = 0.9 * moment + 0.1 * grad
    second_new = 0.95 * second + 0.05 * grad * grad
    corrected = moment_new / (1.0 - 0.9**10)
    scaled = jnp.sqrt(second_new / (1.0 - 0.95**10)) + 1e-08
    param_new = param - 0.01 * (corrected / scaled + 0.1 * param)
    return (param_new, moment_new, second_new)


def update(dense_in, expert_in, dense_out, expert_out, dense_new, expert_new, sem):
    copies = []

    def rows_of(ins, news, outs, first, count):
        span = pl.ds(first, count)
        for new, out, value in zip(news, outs, adamw(*(ref[span] for ref in ins)), strict=True):
            new[span] = value
            copies.append(pltpu.make_async_copy(new.at[span], out.at[span], sem.at[len(copies)]))
            copies[-1].start()

    rows = expert_in[0].shape[0]
    step = rows // STRETCHES
    for i in range(STRETCHES):
        rows_of(expert_in, expert_new, expert_out, i * step, step)
    rows_of(dense_in, dense_new, dense_out, 0, dense_in[0].shape[0])
    for copy in copies:
        copy.wait()


def wave(k):
    half = (k + 1) // 2
    return 4 + half if k % 2 == 0 else 4 - half


def exchange(
    counts_hbm,
    partials,
    inputs,
    outputs,
    grad,
    dense,
    counts,
    ins,
    outs,
    relay_ins,
    relay_outs,
    rows,
    counts_sem,
    send,
    x_out_recv,
    x_in_recv,
    out_recv,
    in_recv,
    row_recv,
    y_recv,
    core_recv,
):
    d, e = lax.axis_index("dp"), lax.axis_index("expert")
    y, c = d // 2, d % 2
    x, z = e // Z, e % Z
    ahead = lax.rem(y + 1 + 2 * c, Y)
    behind = lax.rem(y + 3 - 2 * c, Y)
    across = lax.rem(y + 2, Y)
    sibling = 2 * y + 1 - c
    to_x, to_z, to_y, to_core, to_rows = (send.at[i] for i in range(5))

    def remote(src, dst, send, recv, dp, expert):
        return pltpu.make_async_remote_copy(
            src_ref=src,
            dst_ref=dst,
            send_sem=send,
            recv_sem=recv,
            device_id=(dp, expert),
            device_id_type=MESH,
        )

    def peer(dx, dz):
        return lax.rem(x + dx, X) * Z + lax.rem(z + dz, Z)

    load_counts = pltpu.make_async_copy(counts_hbm, counts, counts_sem)
    load_counts.start()
    barrier = pltpu.get_barrier_semaphore()
    for dz in range(1, Z):
        pl.semaphore_signal(barrier, inc=1, device_id=(d, peer(0, dz)), device_id_type=MESH)
    for dx in range(1, X):
        pl.semaphore_signal(barrier, inc=1, device_id=(d, peer(dx, 0)), device_id_type=MESH)
    for step in range(1, DP):
        pl.semaphore_signal(barrier, inc=1, device_id=(lax.rem(d + step, DP), e), device_id_type=MESH)
    pl.semaphore_wait(barrier, Z - 1 + X - 1 + DP - 1)

    def slot_of(source_z, dx):
        return source_z * X + dx

    def slots_from(k):
        return pl.ds(pl.multiple_of(lax.rem(z + Z - wave(k), Z) * X, X), X)

    def wait_recv(ref, recv):
        remote(ref, ref, recv, recv, d, e).wait_recv()

    def to_columns(k, src_of, buffer, relay, x_recv, recv):
        for dx in (2, 1, 3):
            block = src_of(peer(dx, wave(k)))
            if wave(k):
                remote(block, relay.at[k, dx - 1], to_x, x_recv.at[k], d, peer(dx, 0)).start()
            else:
                remote(block, buffer(pl.ds(slot_of(z, dx), 1)).at[0], to_x, recv.at[k], d, peer(dx, 0)).start()

    def own_column(k, src_of, buffer, recv):
        there = peer(0, wave(k))
        mine = buffer(pl.ds(slot_of(z, 0), 1)).at[0]
        if wave(k):
            remote(src_of(there), mine, to_z, recv.at[k], d, there).start()
        else:
            pltpu.make_async_copy(src_of(there), mine, recv.at[k]).start()

    def relay_column(k, buffer, relay, x_recv, recv):
        if wave(k):
            wait_recv(relay.at[k], x_recv.at[k])
            remote(relay.at[k], buffer(pl.ds(slot_of(z, 1), X - 1)), to_z, recv.at[k], d, peer(0, wave(k))).start()

    def out_src(there):
        return outputs.at[there, d]

    def out_at(slots):
        return outs.at[d, slots]

    def in_src(there):
        return inputs.at[there]

    def in_at(slots):
        return ins.at[slots]

    for k in range(Z):
        own_column(k, out_src, out_at, out_recv)
        to_columns(k, out_src, out_at, relay_outs, x_out_recv, out_recv)
    for step in range(1, DP):
        there = lax.rem(d + step, DP)
        remote(partials.at[there], rows.at[d], to_rows, row_recv, there, e).start()
    pltpu.make_async_copy(partials.at[d], rows.at[d], row_recv).start()

    def own(k):
        piece = outs.at[d, slots_from(k)]
        wait_recv(piece, out_recv.at[k])
        remote(piece, piece, to_y, y_recv.at[k, 0], 2 * ahead + c, e).start()
        remote(piece, piece, to_y, y_recv.at[k, 1], 2 * behind + c, e).start()
        remote(piece, piece, to_core, core_recv.at[k, 0], sibling, e).start()

    def near(k):
        piece = outs.at[2 * behind + c, slots_from(k)]
        wait_recv(piece, y_recv.at[k, 0])
        remote(piece, piece, to_y, y_recv.at[k, 2], 2 * ahead + c, e).start()
        remote(piece, piece, to_core, core_recv.at[k, 1], sibling, e).start()
        piece = outs.at[2 * ahead + c, slots_from(k)]
        wait_recv(piece, y_recv.at[k, 1])
        remote(piece, piece, to_core, core_recv.at[k, 2], sibling, e).start()

    def far(k):
        piece = outs.at[2 * across + c, slots_from(k)]
        wait_recv(piece, y_recv.at[k, 2])
        remote(piece, piece, to_core, core_recv.at[k, 3], sibling, e).start()

    for i in range(Z + 5):
        if i < Z:
            relay_column(i, out_at, relay_outs, x_out_recv, out_recv)
            to_columns(i, in_src, in_at, relay_ins, x_in_recv, in_recv)
        if 3 <= i < Z + 3:
            own(i - 3)
        if 4 <= i < Z + 4:
            own_column(i - 4, in_src, in_at, in_recv)
            relay_column(i - 4, in_at, relay_ins, x_in_recv, in_recv)
            near(i - 4)
        if 5 <= i:
            far(i - 5)

    wait_recv(rows, row_recv)
    total = rows[0]
    for step in range(1, DP):
        total = total + rows[step]
    dense[...] = total
    load_counts.wait()

    for n, k in enumerate((0, 1, 2, 3, 4, 5, 7, 6)):
        slots = slots_from(k)
        wait_recv(outs.at[sibling, slots], core_recv.at[k, 0])
        wait_recv(outs.at[2 * ahead + 1 - c, slots], core_recv.at[k, 1])
        wait_recv(outs.at[2 * behind + 1 - c, slots], core_recv.at[k, 2])
        wait_recv(outs.at[2 * across + 1 - c, slots], core_recv.at[k, 3])
        wait_recv(ins.at[slots], in_recv.at[k])
        from_z = lax.rem(z + Z - wave(k), Z)
        live = []
        for dx in range(X):
            block = ins[slot_of(from_z, dx)]
            slot = BF16_ROWS * lax.broadcasted_iota(jnp.int32, block.shape, 0) + lax.broadcasted_iota(jnp.int32, block.shape, 1)
            count = counts[lax.rem(x + X - dx, X) * Z + from_z, e]
            live.append(jnp.where(slot < count, block, jnp.zeros_like(block)))
        left = jnp.stack(live, axis=1)
        right = outs[:, slots]
        product = lax.dot_general(
            left.reshape(-1, left.shape[-1]),
            right.reshape(-1, right.shape[-1]),
            (((0,), (0,)), ((), ())),
            preferred_element_type=jnp.float32,
        )
        if n == 0:
            grad[...] = product
        else:
            grad[...] += product

    def wait_send(ref, sem):
        remote(ref, ref, sem, sem, d, e).wait_send()

    wait_send(outs.at[0, pl.ds(0, Z * (X - 1))], to_x)
    wait_send(ins.at[pl.ds(0, Z * (X - 1))], to_x)
    wait_send(outs.at[0, pl.ds(0, (Z - 1) * X)], to_z)
    wait_send(ins.at[pl.ds(0, (Z - 1) * X)], to_z)
    wait_send(rows.at[pl.ds(0, DP - 1)], to_rows)
    wait_send(outs.at[pl.ds(0, 3)], to_y)
    wait_send(outs.at[pl.ds(0, 4)], to_core)


def per_device(
    dense_partials,
    dense_param,
    dense_m,
    dense_v,
    sent_inputs,
    sent_outputs,
    counts,
    expert_param,
    expert_m,
    expert_v,
):
    blocks, slots, width_in = sent_inputs.shape
    width_out = sent_outputs.shape[2]
    part = slots // DP
    dense_rows, dense_width = dense_partials.shape[1] // DP, dense_partials.shape[2]
    dma = pltpu.SemaphoreType.DMA
    expert_grad, dense_grad = pl.pallas_call(
        exchange,
        name="exchange",
        out_shape=(
            jax.ShapeDtypeStruct((width_in, width_out), jnp.float32),
            jax.ShapeDtypeStruct((dense_rows, dense_width), jnp.float32),
        ),
        in_specs=[pl.BlockSpec(memory_space=pltpu.HBM)] * 4,
        out_specs=(pl.BlockSpec(memory_space=pltpu.VMEM),) * 2,
        scratch_shapes=[
            pltpu.SMEM(counts.shape, counts.dtype),
            pltpu.VMEM((blocks, DP, part, width_in), jnp.bfloat16),
            pltpu.VMEM((DP, blocks, part, width_out), jnp.bfloat16),
            pltpu.VMEM((Z - 1, X - 1, DP, part, width_in), jnp.bfloat16),
            pltpu.VMEM((Z - 1, X - 1, part, width_out), jnp.bfloat16),
            pltpu.VMEM((DP, dense_rows, dense_width), jnp.float32),
            dma,
            dma((5,)),
            dma((Z - 1,)),
            dma((Z - 1,)),
            dma((Z,)),
            dma((Z,)),
            dma,
            dma((Z, 3)),
            dma((Z, 4)),
        ],
        cost_estimate=pl.CostEstimate(
            flops=2 * blocks * slots * width_in * width_out,
            bytes_accessed=2 * blocks * slots * (width_in + width_out),
            transcendentals=0,
        ),
        compiler_params=pltpu.CompilerParams(collective_id=0, has_side_effects=True, vmem_limit_bytes=48 << 20),
    )(
        *(
            pltpu.with_memory_space_constraint(operand, pltpu.HBM)
            for operand in (
                counts,
                dense_partials.reshape(DP, dense_rows, dense_width),
                sent_inputs.reshape(blocks, DP, part, width_in),
                sent_outputs.reshape(blocks, DP, part, width_out),
            )
        )
    )
    dense_state = (dense_param, dense_m, dense_v)
    expert_state = tuple(leaf[0] for leaf in (expert_param, expert_m, expert_v))
    dense_new, expert_new = pl.pallas_call(
        update,
        name="update",
        out_shape=tuple(tuple(jax.ShapeDtypeStruct(leaf.shape, leaf.dtype) for leaf in state) for state in (dense_state, expert_state)),
        in_specs=((pl.BlockSpec(memory_space=pltpu.VMEM),) * 4,) * 2,
        out_specs=((pl.BlockSpec(memory_space=pl.ANY),) * 3,) * 2,
        scratch_shapes=[
            tuple(pltpu.VMEM(leaf.shape, leaf.dtype) for leaf in dense_state),
            tuple(pltpu.VMEM(leaf.shape, leaf.dtype) for leaf in expert_state),
            dma((3 * (STRETCHES + 1),)),
        ],
        compiler_params=pltpu.CompilerParams(vmem_limit_bytes=24 << 20),
    )((*dense_state, dense_grad), (*expert_state, expert_grad))
    return (*dense_new, *(leaf[None] for leaf in expert_new))


def solution(mesh):
    in_specs = (
        P("dp", None, "expert"),
        P("dp", "expert"),
        P("dp", "expert"),
        P("dp", "expert"),
        P("expert", None, "dp"),
        P("expert", None, None),
        P(),
        P("expert", "dp", None),
        P("expert", "dp", None),
        P("expert", "dp", None),
    )
    out_specs = (
        P("dp", "expert"),
        P("dp", "expert"),
        P("dp", "expert"),
        P("expert", "dp", None),
        P("expert", "dp", None),
        P("expert", "dp", None),
    )
    return jax.shard_map(per_device, mesh=mesh, in_specs=in_specs, out_specs=out_specs, check_vma=False)
```

```python
import jax
import jax.numpy as jnp
from jax import lax
from jax.experimental import pallas as pl
from jax.experimental.pallas import tpu as pltpu
from jax.sharding import PartitionSpec as P

MESH = pl.DeviceIdType.MESH
X, Z, Y = 4, 8, 4
DP = 2 * Y
BF16_ROWS = 16
STRETCHES = 8


def adamw(param, moment, second, grad):
    moment_new = 0.9 * moment + 0.1 * grad
    second_new = 0.95 * second + (0.05 * grad) * grad
    scaled = jnp.sqrt(second_new * (1.0 / (1.0 - 0.95**10))) + 1e-08
    param_new = (1.0 - 0.01 * 0.1) * param - (0.01 / (1.0 - 0.9**10)) * moment_new / scaled
    return (param_new, moment_new, second_new)


def update(dense_in, expert_in, dense_out, expert_out, dense_new, expert_new, sem):
    copies = []

    def rows_of(ins, news, outs, first, count):
        span = pl.ds(first, count)
        for new, out, value in zip(news, outs, adamw(*(ref[span] for ref in ins)), strict=True):
            new[span] = value
            copies.append(pltpu.make_async_copy(new.at[span], out.at[span], sem.at[len(copies)]))
            copies[-1].start()

    rows = expert_in[0].shape[0]
    step = rows // STRETCHES
    for i in range(STRETCHES):
        rows_of(expert_in, expert_new, expert_out, i * step, step)
    rows_of(dense_in, dense_new, dense_out, 0, dense_in[0].shape[0])
    for copy in copies:
        copy.wait()


def wave(k):
    half = (k + 1) // 2
    return 4 + half if k % 2 == 0 else 4 - half


TAIL = (5, 6)


def exchange(
    counts_hbm,
    partials,
    inputs,
    outputs,
    grad,
    dense,
    counts,
    ins,
    outs,
    relay_ins,
    relay_outs,
    rows,
    rows_core,
    rows_hop,
    counts_sem,
    send,
    x_out_recv,
    x_in_recv,
    out_recv,
    in_recv,
    tail_recv,
    row_recv,
    hop_recv,
    y_recv,
    core_recv,
):
    d, e = lax.axis_index("dp"), lax.axis_index("expert")
    y, c = d // 2, d % 2
    x, z = e // Z, e % Z
    ahead = lax.rem(y + 1 + 2 * c, Y)
    behind = lax.rem(y + 3 - 2 * c, Y)
    across = lax.rem(y + 2, Y)
    sibling = 2 * y + 1 - c
    to_x, to_z, to_y, to_core, to_rows = (send.at[i] for i in range(5))

    def remote(src, dst, send, recv, dp, expert):
        return pltpu.make_async_remote_copy(
            src_ref=src,
            dst_ref=dst,
            send_sem=send,
            recv_sem=recv,
            device_id=(dp, expert),
            device_id_type=MESH,
        )

    def peer(dx, dz):
        return lax.rem(x + dx, X) * Z + lax.rem(z + dz, Z)

    load_counts = pltpu.make_async_copy(counts_hbm, counts, counts_sem)
    load_counts.start()
    barrier = pltpu.get_barrier_semaphore()
    for dz in range(1, Z):
        pl.semaphore_signal(barrier, inc=1, device_id=(d, peer(0, dz)), device_id_type=MESH)
    for dx in range(1, X):
        pl.semaphore_signal(barrier, inc=1, device_id=(d, peer(dx, 0)), device_id_type=MESH)
    for there in (2 * ahead + c, 2 * behind + c, sibling):
        pl.semaphore_signal(barrier, inc=1, device_id=(there, e), device_id_type=MESH)
    pl.semaphore_wait(barrier, Z - 1 + X - 1 + 3)

    def slot_of(source_z, dx):
        return source_z * X + dx

    def slots_from(k):
        return pl.ds(pl.multiple_of(lax.rem(z + Z - wave(k), Z) * X, X), X)

    def wait_recv(ref, recv):
        remote(ref, ref, recv, recv, d, e).wait_recv()

    def to_columns(k, src_of, buffer, relay, x_recv, recv):
        for dx in (2, 1, 3):
            block = src_of(peer(dx, wave(k)))
            if wave(k):
                remote(block, relay.at[k, dx - 1], to_x, x_recv.at[k], d, peer(dx, 0)).start()
            else:
                remote(block, buffer(pl.ds(slot_of(z, dx), 1)).at[0], to_x, recv.at[k], d, peer(dx, 0)).start()

    def own_column(k, src_of, buffer, recv):
        there = peer(0, wave(k))
        mine = buffer(pl.ds(slot_of(z, 0), 1)).at[0]
        if wave(k):
            remote(src_of(there), mine, to_z, recv.at[k], d, there).start()
        else:
            pltpu.make_async_copy(src_of(there), mine, recv.at[k]).start()

    def relay_column(k, buffer, relay, x_recv, recv):
        if wave(k):
            wait_recv(relay.at[k], x_recv.at[k])
            remote(relay.at[k], buffer(pl.ds(slot_of(z, 1), X - 1)), to_z, recv.at[k], d, peer(0, wave(k))).start()

    def out_src(there):
        return outputs.at[there, d]

    def out_at(slots):
        return outs.at[d, slots]

    def in_src(there):
        return inputs.at[there]

    def in_at(slots):
        return ins.at[slots]

    for k in range(Z):
        own_column(k, out_src, out_at, out_recv)
        to_columns(k, out_src, out_at, relay_outs, x_out_recv, out_recv)
    remote(partials.at[:, 1 - c], rows_core, to_rows, row_recv.at[0], sibling, e).start()
    own_rows = pltpu.make_async_copy(partials.at[:, c], rows, row_recv.at[1])
    own_rows.start()

    def rows_of_chip():
        own_rows.wait()
        wait_recv(rows_core, row_recv.at[0])
        rows[...] += rows_core[...]
        remote(rows.at[across], rows_hop.at[0], to_rows, hop_recv.at[0], 2 * ahead + c, e).start()
        remote(rows.at[behind], rows_hop.at[1], to_rows, hop_recv.at[1], 2 * behind + c, e).start()

    def rows_of_two_chips():
        wait_recv(rows_hop.at[0], hop_recv.at[0])
        rows[ahead] += rows_hop[0]
        remote(rows.at[ahead], rows_hop.at[2], to_rows, hop_recv.at[2], 2 * ahead + c, e).start()

    def own(k):
        piece = outs.at[d, slots_from(k)]
        wait_recv(piece, out_recv.at[k])
        remote(piece, piece, to_y, y_recv.at[k, 0], 2 * ahead + c, e).start()
        remote(piece, piece, to_y, y_recv.at[k, 1], 2 * behind + c, e).start()
        remote(piece, piece, to_core, core_recv.at[k, 0], sibling, e).start()

    def near(k):
        piece = outs.at[2 * behind + c, slots_from(k)]
        wait_recv(piece, y_recv.at[k, 0])
        remote(piece, piece, to_y, y_recv.at[k, 2], 2 * ahead + c, e).start()
        remote(piece, piece, to_core, core_recv.at[k, 1], sibling, e).start()
        piece = outs.at[2 * ahead + c, slots_from(k)]
        wait_recv(piece, y_recv.at[k, 1])
        remote(piece, piece, to_core, core_recv.at[k, 2], sibling, e).start()

    def far(k):
        piece = outs.at[2 * across + c, slots_from(k)]
        wait_recv(piece, y_recv.at[k, 2])
        remote(piece, piece, to_core, core_recv.at[k, 3], sibling, e).start()

    def send_tail(k):
        there = peer(0, wave(k))
        recv = tail_recv.at[k - TAIL[0]]
        remote(in_src(there), ins.at[slot_of(z, 0)], to_z, recv.at[0], d, there).start()
        wait_recv(relay_ins.at[k], x_in_recv.at[k])
        for dx in range(1, X):
            remote(relay_ins.at[k, dx - 1], ins.at[slot_of(z, dx)], to_z, recv.at[dx], d, there).start()

    for i in range(Z + 5):
        if i < Z:
            relay_column(i, out_at, relay_outs, x_out_recv, out_recv)
            to_columns(i, in_src, in_at, relay_ins, x_in_recv, in_recv)
        if 3 <= i < Z + 3:
            own(i - 3)
        if 4 <= i < Z + 4:
            if i - 4 in TAIL:
                send_tail(i - 4)
            else:
                own_column(i - 4, in_src, in_at, in_recv)
                relay_column(i - 4, in_at, relay_ins, x_in_recv, in_recv)
            near(i - 4)
        if 5 <= i:
            far(i - 5)
        if i == 2:
            rows_of_chip()
        if i == 4:
            rows_of_two_chips()

    wait_recv(rows_hop.at[1], hop_recv.at[1])
    wait_recv(rows_hop.at[2], hop_recv.at[2])
    dense[...] = (rows[y] + rows_hop[1]) + rows_hop[2]
    load_counts.wait()

    def gathered(k):
        slots = slots_from(k)
        wait_recv(outs.at[sibling, slots], core_recv.at[k, 0])
        wait_recv(outs.at[2 * ahead + 1 - c, slots], core_recv.at[k, 1])
        wait_recv(outs.at[2 * behind + 1 - c, slots], core_recv.at[k, 2])
        wait_recv(outs.at[2 * across + 1 - c, slots], core_recv.at[k, 3])

    def product(pieces):
        left, right = [], []
        for k, dx in pieces:
            from_z = lax.rem(z + Z - wave(k), Z)
            block = ins[slot_of(from_z, dx)]
            slot = BF16_ROWS * lax.broadcasted_iota(jnp.int32, block.shape, 0) + lax.broadcasted_iota(jnp.int32, block.shape, 1)
            count = counts[lax.rem(x + X - dx, X) * Z + from_z, e]
            left.append(jnp.where(slot < count, block, jnp.zeros_like(block)).reshape(-1, block.shape[-1]))
            right.append(outs[:, slot_of(from_z, dx)].reshape(-1, outs.shape[-1]))
        return lax.dot_general(
            jnp.concatenate(left, axis=0),
            jnp.concatenate(right, axis=0),
            (((0,), (0,)), ((), ())),
            preferred_element_type=jnp.float32,
        )

    for k in (0, 1, 2, 3, 4, 7):
        gathered(k)
        wait_recv(ins.at[slots_from(k)], in_recv.at[k])
        if k == 0:
            grad[...] = product([(k, dx) for dx in range(X)])
        else:
            grad[...] += product([(k, dx) for dx in range(X)])
    for k in TAIL:
        gathered(k)
    for dx in range(X):
        for k in TAIL:
            piece = slot_of(lax.rem(z + Z - wave(k), Z), dx)
            wait_recv(ins.at[piece], tail_recv.at[k - TAIL[0], dx])
        grad[...] += product([(k, dx) for k in TAIL])

    def wait_send(ref, sem):
        remote(ref, ref, sem, sem, d, e).wait_send()

    wait_send(outs.at[0, pl.ds(0, Z * (X - 1))], to_x)
    wait_send(ins.at[pl.ds(0, Z * (X - 1))], to_x)
    wait_send(outs.at[0, pl.ds(0, (Z - 1) * X)], to_z)
    wait_send(ins.at[pl.ds(0, (Z - 1) * X)], to_z)
    wait_send(rows, to_rows)
    wait_send(rows_hop, to_rows)
    wait_send(outs.at[pl.ds(0, 3)], to_y)
    wait_send(outs.at[pl.ds(0, 4)], to_core)


def per_device(
    dense_partials,
    dense_param,
    dense_m,
    dense_v,
    sent_inputs,
    sent_outputs,
    counts,
    expert_param,
    expert_m,
    expert_v,
):
    blocks, slots, width_in = sent_inputs.shape
    width_out = sent_outputs.shape[2]
    part = slots // DP
    dense_rows, dense_width = dense_partials.shape[1] // DP, dense_partials.shape[2]
    dma = pltpu.SemaphoreType.DMA
    expert_grad, dense_grad = pl.pallas_call(
        exchange,
        name="exchange",
        out_shape=(
            jax.ShapeDtypeStruct((width_in, width_out), jnp.float32),
            jax.ShapeDtypeStruct((dense_rows, dense_width), jnp.float32),
        ),
        in_specs=[pl.BlockSpec(memory_space=pltpu.HBM)] * 4,
        out_specs=(pl.BlockSpec(memory_space=pltpu.VMEM),) * 2,
        scratch_shapes=[
            pltpu.SMEM(counts.shape, counts.dtype),
            pltpu.VMEM((blocks, DP, part, width_in), jnp.bfloat16),
            pltpu.VMEM((DP, blocks, part, width_out), jnp.bfloat16),
            pltpu.VMEM((Z - 1, X - 1, DP, part, width_in), jnp.bfloat16),
            pltpu.VMEM((Z - 1, X - 1, part, width_out), jnp.bfloat16),
            pltpu.VMEM((Y, dense_rows, dense_width), jnp.float32),
            pltpu.VMEM((Y, dense_rows, dense_width), jnp.float32),
            pltpu.VMEM((3, dense_rows, dense_width), jnp.float32),
            dma,
            dma((5,)),
            dma((Z - 1,)),
            dma((Z - 1,)),
            dma((Z,)),
            dma((Z,)),
            dma((len(TAIL), X)),
            dma((2,)),
            dma((3,)),
            dma((Z, 3)),
            dma((Z, 4)),
        ],
        cost_estimate=pl.CostEstimate(
            flops=2 * blocks * slots * width_in * width_out,
            bytes_accessed=2 * blocks * slots * (width_in + width_out),
            transcendentals=0,
        ),
        compiler_params=pltpu.CompilerParams(collective_id=0, has_side_effects=True, vmem_limit_bytes=48 << 20),
    )(
        *(
            pltpu.with_memory_space_constraint(operand, pltpu.HBM)
            for operand in (
                counts,
                dense_partials.reshape(Y, 2, dense_rows, dense_width),
                sent_inputs.reshape(blocks, DP, part, width_in),
                sent_outputs.reshape(blocks, DP, part, width_out),
            )
        )
    )
    dense_state = (dense_param, dense_m, dense_v)
    expert_state = tuple(leaf[0] for leaf in (expert_param, expert_m, expert_v))
    dense_new, expert_new = pl.pallas_call(
        update,
        name="update",
        out_shape=tuple(tuple(jax.ShapeDtypeStruct(leaf.shape, leaf.dtype) for leaf in state) for state in (dense_state, expert_state)),
        in_specs=((pl.BlockSpec(memory_space=pltpu.VMEM),) * 4,) * 2,
        out_specs=((pl.BlockSpec(memory_space=pl.ANY),) * 3,) * 2,
        scratch_shapes=[
            tuple(pltpu.VMEM(leaf.shape, leaf.dtype) for leaf in dense_state),
            tuple(pltpu.VMEM(leaf.shape, leaf.dtype) for leaf in expert_state),
            dma((3 * (STRETCHES + 1),)),
        ],
        compiler_params=pltpu.CompilerParams(vmem_limit_bytes=24 << 20),
    )((*dense_state, dense_grad), (*expert_state, expert_grad))
    return (*dense_new, *(leaf[None] for leaf in expert_new))


def solution(mesh):
    in_specs = (
        P("dp", None, "expert"),
        P("dp", "expert"),
        P("dp", "expert"),
        P("dp", "expert"),
        P("expert", None, "dp"),
        P("expert", None, None),
        P(),
        P("expert", "dp", None),
        P("expert", "dp", None),
        P("expert", "dp", None),
    )
    out_specs = (
        P("dp", "expert"),
        P("dp", "expert"),
        P("dp", "expert"),
        P("expert", "dp", None),
        P("expert", "dp", None),
        P("expert", "dp", None),
    )
    return jax.shard_map(per_device, mesh=mesh, in_specs=in_specs, out_specs=out_specs, check_vma=False)
```

```python
import jax
import jax.numpy as jnp
from jax import lax
from jax.experimental import pallas as pl
from jax.experimental.pallas import tpu as pltpu
from jax.sharding import PartitionSpec as P

MESH = pl.DeviceIdType.MESH
X, Z, Y = 4, 8, 4
DP = 2 * Y
BF16_ROWS = 16
STRETCHES = (2, 4, 6, 8, 12)


def adamw(param, moment, second, grad):
    moment_new = 0.9 * moment + 0.1 * grad
    second_new = 0.95 * second + (0.05 * grad) * grad
    scaled = jnp.sqrt(second_new * (1.0 / (1.0 - 0.95**10))) + 1e-08
    param_new = (1.0 - 0.01 * 0.1) * param - (0.01 / (1.0 - 0.9**10)) * moment_new / scaled
    return (param_new, moment_new, second_new)


def update(dense_in, expert_in, dense_out, expert_out, dense_new, expert_new, sem):
    copies = []

    def rows_of(ins, news, outs, first, count):
        span = pl.ds(first, count)
        for new, out, value in zip(news, outs, adamw(*(ref[span] for ref in ins)), strict=True):
            new[span] = value
            copies.append(pltpu.make_async_copy(new.at[span], out.at[span], sem.at[len(copies)]))
            copies[-1].start()

    rows_of(dense_in, dense_new, dense_out, 0, dense_in[0].shape[0])
    first = 0
    for groups in STRETCHES:
        rows_of(expert_in, expert_new, expert_out, first, 8 * groups)
        first += 8 * groups
    for copy in copies:
        copy.wait()


def wave(k):
    half = (k + 1) // 2
    return 4 + half if k % 2 == 0 else 4 - half


TAIL = (5, 6)


def exchange(
    counts_hbm,
    partials,
    inputs,
    outputs,
    grad,
    dense,
    counts,
    ins,
    outs,
    relay_ins,
    relay_outs,
    rows,
    rows_core,
    rows_hop,
    counts_sem,
    send,
    x_out_recv,
    x_in_recv,
    out_recv,
    in_recv,
    tail_recv,
    row_recv,
    hop_recv,
    y_recv,
    core_recv,
):
    d, e = lax.axis_index("dp"), lax.axis_index("expert")
    y, c = d // 2, d % 2
    x, z = e // Z, e % Z
    ahead = lax.rem(y + 1 + 2 * c, Y)
    behind = lax.rem(y + 3 - 2 * c, Y)
    across = lax.rem(y + 2, Y)
    sibling = 2 * y + 1 - c
    to_x, to_z, to_y, to_core, to_rows = (send.at[i] for i in range(5))

    def remote(src, dst, send, recv, dp, expert):
        return pltpu.make_async_remote_copy(
            src_ref=src,
            dst_ref=dst,
            send_sem=send,
            recv_sem=recv,
            device_id=(dp, expert),
            device_id_type=MESH,
        )

    def peer(dx, dz):
        return lax.rem(x + dx, X) * Z + lax.rem(z + dz, Z)

    barrier = pltpu.get_barrier_semaphore()
    for dz in (4, 3, 5, 2, 6, 1, 7):
        pl.semaphore_signal(barrier, inc=1, device_id=(d, peer(0, dz)), device_id_type=MESH)
    for dx in (2, 1, 3):
        pl.semaphore_signal(barrier, inc=1, device_id=(d, peer(dx, 0)), device_id_type=MESH)
    for there in (2 * ahead + c, 2 * behind + c, sibling):
        pl.semaphore_signal(barrier, inc=1, device_id=(there, e), device_id_type=MESH)
    slot = z * X
    load_counts = pltpu.make_async_copy(counts_hbm, counts, counts_sem)
    own_rows = pltpu.make_async_copy(partials.at[:, c], rows, row_recv.at[1])
    own_outs = pltpu.make_async_copy(outputs.at[e, d], outs.at[d, slot], out_recv.at[Z - 1])
    own_ins = pltpu.make_async_copy(inputs.at[e], ins.at[slot], in_recv.at[Z - 1])
    for copy in (load_counts, own_rows, own_outs, own_ins):
        copy.start()
    pl.semaphore_wait(barrier, Z - 1 + X - 1 + 3)

    def slot_of(source_z, dx):
        return source_z * X + dx

    def slots_from(k):
        return pl.ds(pl.multiple_of(lax.rem(z + Z - wave(k), Z) * X, X), X)

    def wait_recv(ref, recv):
        remote(ref, ref, recv, recv, d, e).wait_recv()

    def to_columns(k, src_of, buffer, relay, x_recv, recv):
        for dx in (2, 1, 3):
            block = src_of(peer(dx, wave(k)))
            if wave(k):
                remote(block, relay.at[k, dx - 1], to_x, x_recv.at[k], d, peer(dx, 0)).start()
            else:
                remote(block, buffer(pl.ds(slot_of(z, dx), 1)).at[0], to_x, recv.at[k], d, peer(dx, 0)).start()

    def own_column(k, src_of, buffer, recv):
        there = peer(0, wave(k))
        mine = buffer(pl.ds(slot_of(z, 0), 1)).at[0]
        if wave(k):
            remote(src_of(there), mine, to_z, recv.at[k], d, there).start()

    def relay_column(k, buffer, relay, x_recv, recv):
        if wave(k):
            wait_recv(relay.at[k], x_recv.at[k])
            remote(relay.at[k], buffer(pl.ds(slot_of(z, 1), X - 1)), to_z, recv.at[k], d, peer(0, wave(k))).start()

    def out_src(there):
        return outputs.at[there, d]

    def out_at(slots):
        return outs.at[d, slots]

    def in_src(there):
        return inputs.at[there]

    def in_at(slots):
        return ins.at[slots]

    for k in range(Z):
        own_column(k, out_src, out_at, out_recv)
        to_columns(k, out_src, out_at, relay_outs, x_out_recv, out_recv)
    remote(partials.at[:, 1 - c], rows_core, to_rows, row_recv.at[0], sibling, e).start()

    def rows_of_chip():
        own_rows.wait()
        wait_recv(rows_core, row_recv.at[0])
        rows[...] += rows_core[...]
        remote(rows.at[across], rows_hop.at[0], to_rows, hop_recv.at[0], 2 * ahead + c, e).start()
        remote(rows.at[behind], rows_hop.at[1], to_rows, hop_recv.at[1], 2 * behind + c, e).start()

    def rows_of_two_chips():
        wait_recv(rows_hop.at[0], hop_recv.at[0])
        rows[ahead] += rows_hop[0]
        remote(rows.at[ahead], rows_hop.at[2], to_rows, hop_recv.at[2], 2 * ahead + c, e).start()

    def own(k):
        piece = outs.at[d, slots_from(k)]
        wait_recv(piece, out_recv.at[k])
        remote(piece, piece, to_y, y_recv.at[k, 0], 2 * ahead + c, e).start()
        remote(piece, piece, to_y, y_recv.at[k, 1], 2 * behind + c, e).start()
        remote(piece, piece, to_core, core_recv.at[k, 0], sibling, e).start()

    def near(k):
        piece = outs.at[2 * behind + c, slots_from(k)]
        wait_recv(piece, y_recv.at[k, 0])
        remote(piece, piece, to_y, y_recv.at[k, 2], 2 * ahead + c, e).start()
        remote(piece, piece, to_core, core_recv.at[k, 1], sibling, e).start()
        piece = outs.at[2 * ahead + c, slots_from(k)]
        wait_recv(piece, y_recv.at[k, 1])
        remote(piece, piece, to_core, core_recv.at[k, 2], sibling, e).start()

    def far(k):
        piece = outs.at[2 * across + c, slots_from(k)]
        wait_recv(piece, y_recv.at[k, 2])
        remote(piece, piece, to_core, core_recv.at[k, 3], sibling, e).start()

    def send_tail(k):
        there = peer(0, wave(k))
        recv = tail_recv.at[k - TAIL[0]]
        remote(in_src(there), ins.at[slot_of(z, 0)], to_z, recv.at[0], d, there).start()
        wait_recv(relay_ins.at[k], x_in_recv.at[k])
        for dx in range(1, X):
            remote(relay_ins.at[k, dx - 1], ins.at[slot_of(z, dx)], to_z, recv.at[dx], d, there).start()

    for i in range(Z + 5):
        if i < Z:
            relay_column(i, out_at, relay_outs, x_out_recv, out_recv)
            to_columns(i, in_src, in_at, relay_ins, x_in_recv, in_recv)
        if 3 <= i < Z + 3:
            own(i - 3)
        if 4 <= i < Z + 4:
            if i - 4 in TAIL:
                send_tail(i - 4)
            else:
                own_column(i - 4, in_src, in_at, in_recv)
                relay_column(i - 4, in_at, relay_ins, x_in_recv, in_recv)
            near(i - 4)
        if 5 <= i:
            far(i - 5)
        if i == 2:
            rows_of_chip()
        if i == 4:
            rows_of_two_chips()

    wait_recv(rows_hop.at[1], hop_recv.at[1])
    wait_recv(rows_hop.at[2], hop_recv.at[2])
    dense[...] = (rows[y] + rows_hop[1]) + rows_hop[2]
    load_counts.wait()

    def gathered(k):
        slots = slots_from(k)
        wait_recv(outs.at[sibling, slots], core_recv.at[k, 0])
        wait_recv(outs.at[2 * ahead + 1 - c, slots], core_recv.at[k, 1])
        wait_recv(outs.at[2 * behind + 1 - c, slots], core_recv.at[k, 2])
        wait_recv(outs.at[2 * across + 1 - c, slots], core_recv.at[k, 3])

    def product(pieces):
        left, right = [], []
        for k, dx in pieces:
            from_z = lax.rem(z + Z - wave(k), Z)
            block = ins[slot_of(from_z, dx)]
            slot = BF16_ROWS * lax.broadcasted_iota(jnp.int32, block.shape, 0) + lax.broadcasted_iota(jnp.int32, block.shape, 1)
            count = counts[lax.rem(x + X - dx, X) * Z + from_z, e]
            left.append(jnp.where(slot < count, block, jnp.zeros_like(block)).reshape(-1, block.shape[-1]))
            right.append(outs[:, slot_of(from_z, dx)].reshape(-1, outs.shape[-1]))
        return lax.dot_general(
            jnp.concatenate(left, axis=0),
            jnp.concatenate(right, axis=0),
            (((0,), (0,)), ((), ())),
            preferred_element_type=jnp.float32,
        )

    for k in (0, 1, 2, 3, 4, 7):
        gathered(k)
        wait_recv(ins.at[slots_from(k)], in_recv.at[k])
        if k == 0:
            grad[...] = product([(k, dx) for dx in range(X)])
        else:
            grad[...] += product([(k, dx) for dx in range(X)])
    for k in TAIL:
        gathered(k)
    for dx in range(X):
        for k in TAIL:
            piece = slot_of(lax.rem(z + Z - wave(k), Z), dx)
            wait_recv(ins.at[piece], tail_recv.at[k - TAIL[0], dx])
        grad[...] += product([(k, dx) for k in TAIL])

    def wait_send(ref, sem):
        remote(ref, ref, sem, sem, d, e).wait_send()

    wait_send(outs.at[0, pl.ds(0, Z * (X - 1))], to_x)
    wait_send(ins.at[pl.ds(0, Z * (X - 1))], to_x)
    wait_send(outs.at[0, pl.ds(0, (Z - 1) * X)], to_z)
    wait_send(ins.at[pl.ds(0, (Z - 1) * X)], to_z)
    wait_send(rows, to_rows)
    wait_send(rows_hop, to_rows)
    wait_send(outs.at[pl.ds(0, 3)], to_y)
    wait_send(outs.at[pl.ds(0, 4)], to_core)


def per_device(
    dense_partials,
    dense_param,
    dense_m,
    dense_v,
    sent_inputs,
    sent_outputs,
    counts,
    expert_param,
    expert_m,
    expert_v,
):
    blocks, slots, width_in = sent_inputs.shape
    width_out = sent_outputs.shape[2]
    part = slots // DP
    dense_rows, dense_width = dense_partials.shape[1] // DP, dense_partials.shape[2]
    dma = pltpu.SemaphoreType.DMA
    expert_grad, dense_grad = pl.pallas_call(
        exchange,
        name="exchange",
        out_shape=(
            jax.ShapeDtypeStruct((width_in, width_out), jnp.float32),
            jax.ShapeDtypeStruct((dense_rows, dense_width), jnp.float32),
        ),
        in_specs=[pl.BlockSpec(memory_space=pltpu.HBM)] * 4,
        out_specs=(pl.BlockSpec(memory_space=pltpu.VMEM),) * 2,
        scratch_shapes=[
            pltpu.SMEM(counts.shape, counts.dtype),
            pltpu.VMEM((blocks, DP, part, width_in), jnp.bfloat16),
            pltpu.VMEM((DP, blocks, part, width_out), jnp.bfloat16),
            pltpu.VMEM((Z - 1, X - 1, DP, part, width_in), jnp.bfloat16),
            pltpu.VMEM((Z - 1, X - 1, part, width_out), jnp.bfloat16),
            pltpu.VMEM((Y, dense_rows, dense_width), jnp.float32),
            pltpu.VMEM((Y, dense_rows, dense_width), jnp.float32),
            pltpu.VMEM((3, dense_rows, dense_width), jnp.float32),
            dma,
            dma((5,)),
            dma((Z - 1,)),
            dma((Z - 1,)),
            dma((Z,)),
            dma((Z,)),
            dma((len(TAIL), X)),
            dma((2,)),
            dma((3,)),
            dma((Z, 3)),
            dma((Z, 4)),
        ],
        cost_estimate=pl.CostEstimate(
            flops=2 * blocks * slots * width_in * width_out,
            bytes_accessed=2 * blocks * slots * (width_in + width_out),
            transcendentals=0,
        ),
        compiler_params=pltpu.CompilerParams(collective_id=0, has_side_effects=True, vmem_limit_bytes=48 << 20),
    )(
        *(
            pltpu.with_memory_space_constraint(operand, pltpu.HBM)
            for operand in (
                counts,
                dense_partials.reshape(Y, 2, dense_rows, dense_width),
                sent_inputs.reshape(blocks, DP, part, width_in),
                sent_outputs.reshape(blocks, DP, part, width_out),
            )
        )
    )
    dense_state = (dense_param, dense_m, dense_v)
    expert_state = tuple(leaf[0] for leaf in (expert_param, expert_m, expert_v))
    dense_new, expert_new = pl.pallas_call(
        update,
        name="update",
        out_shape=tuple(tuple(jax.ShapeDtypeStruct(leaf.shape, leaf.dtype) for leaf in state) for state in (dense_state, expert_state)),
        in_specs=((pl.BlockSpec(memory_space=pltpu.VMEM),) * 4,) * 2,
        out_specs=((pl.BlockSpec(memory_space=pl.ANY),) * 3,) * 2,
        scratch_shapes=[
            tuple(pltpu.VMEM(leaf.shape, leaf.dtype) for leaf in dense_state),
            tuple(pltpu.VMEM(leaf.shape, leaf.dtype) for leaf in expert_state),
            dma((3 * (len(STRETCHES) + 1),)),
        ],
        compiler_params=pltpu.CompilerParams(vmem_limit_bytes=24 << 20),
    )((*dense_state, dense_grad), (*expert_state, expert_grad))
    return (*dense_new, *(leaf[None] for leaf in expert_new))


def solution(mesh):
    in_specs = (
        P("dp", None, "expert"),
        P("dp", "expert"),
        P("dp", "expert"),
        P("dp", "expert"),
        P("expert", None, "dp"),
        P("expert", None, None),
        P(),
        P("expert", "dp", None),
        P("expert", "dp", None),
        P("expert", "dp", None),
    )
    out_specs = (
        P("dp", "expert"),
        P("dp", "expert"),
        P("dp", "expert"),
        P("expert", "dp", None),
        P("expert", "dp", None),
        P("expert", "dp", None),
    )
    return jax.shard_map(per_device, mesh=mesh, in_specs=in_specs, out_specs=out_specs, check_vma=False)
```

```python
import jax
import jax.numpy as jnp
from jax import lax
from jax.experimental import pallas as pl
from jax.experimental.pallas import tpu as pltpu
from jax.sharding import PartitionSpec as P

MESH = pl.DeviceIdType.MESH
X, Z, Y = 4, 8, 4
DP = 2 * Y
BF16_ROWS = 16
STRETCHES = (2, 4, 6, 8, 12)


def adamw(param, moment, second, grad):
    moment_new = 0.9 * moment + 0.1 * grad
    second_new = 0.95 * second + (0.05 * grad) * grad
    scaled = jnp.sqrt(second_new * (1.0 / (1.0 - 0.95**10))) + 1e-08
    param_new = (1.0 - 0.01 * 0.1) * param - (0.01 / (1.0 - 0.9**10)) * moment_new / scaled
    return (param_new, moment_new, second_new)


def update(dense_in, expert_in, dense_out, expert_out, dense_new, expert_new, sem):
    copies = []

    def rows_of(ins, news, outs, first, count):
        span = pl.ds(first, count)
        for new, out, value in zip(news, outs, adamw(*(ref[span] for ref in ins)), strict=True):
            new[span] = value
            copies.append(pltpu.make_async_copy(new.at[span], out.at[span], sem.at[len(copies)]))
            copies[-1].start()

    rows_of(dense_in, dense_new, dense_out, 0, dense_in[0].shape[0])
    first = 0
    for groups in STRETCHES:
        rows_of(expert_in, expert_new, expert_out, first, 8 * groups)
        first += 8 * groups
    for copy in copies:
        copy.wait()


def wave(k):
    half = (k + 1) // 2
    return 4 + half if k % 2 == 0 else 4 - half


TAIL = (5, 6)


def exchange(
    counts_hbm,
    partials,
    inputs,
    outputs,
    grad,
    dense,
    counts,
    ins,
    outs,
    relay_ins,
    relay_outs,
    rows,
    rows_core,
    rows_hop,
    counts_sem,
    send,
    x_out_recv,
    x_in_recv,
    out_recv,
    in_recv,
    tail_recv,
    row_recv,
    hop_recv,
    y_recv,
    core_recv,
):
    d, e = lax.axis_index("dp"), lax.axis_index("expert")
    y, c = d // 2, d % 2
    x, z = e // Z, e % Z
    ahead = lax.rem(y + 1 + 2 * c, Y)
    behind = lax.rem(y + 3 - 2 * c, Y)
    across = lax.rem(y + 2, Y)
    sibling = 2 * y + 1 - c
    to_x, to_z, to_y, to_core, to_rows = (send.at[i] for i in range(5))

    def remote(src, dst, send, recv, dp, expert):
        return pltpu.make_async_remote_copy(
            src_ref=src,
            dst_ref=dst,
            send_sem=send,
            recv_sem=recv,
            device_id=(dp, expert),
            device_id_type=MESH,
        )

    def peer(dx, dz):
        return lax.rem(x + dx, X) * Z + lax.rem(z + dz, Z)

    barrier = pltpu.get_barrier_semaphore()
    for dz in (4, 3, 5, 2, 6, 1, 7):
        pl.semaphore_signal(barrier, inc=1, device_id=(d, peer(0, dz)), device_id_type=MESH)
    for dx in (2, 1, 3):
        pl.semaphore_signal(barrier, inc=1, device_id=(d, peer(dx, 0)), device_id_type=MESH)
    for there in (2 * ahead + c, 2 * behind + c, sibling):
        pl.semaphore_signal(barrier, inc=1, device_id=(there, e), device_id_type=MESH)
    slot = z * X
    load_counts = pltpu.make_async_copy(counts_hbm, counts, counts_sem)
    own_rows = pltpu.make_async_copy(partials.at[:, c], rows, row_recv.at[1])
    own_outs = pltpu.make_async_copy(outputs.at[e, d], outs.at[d, slot], out_recv.at[Z - 1])
    own_ins = pltpu.make_async_copy(inputs.at[e], ins.at[slot], in_recv.at[Z - 1])
    for copy in (load_counts, own_rows, own_outs, own_ins):
        copy.start()
    pl.semaphore_wait(barrier, Z - 1 + X - 1 + 3)

    def slot_of(source_z, dx):
        return source_z * X + dx

    def slots_from(k):
        return pl.ds(pl.multiple_of(lax.rem(z + Z - wave(k), Z) * X, X), X)

    def wait_recv(ref, recv):
        remote(ref, ref, recv, recv, d, e).wait_recv()

    def to_columns(k, src_of, buffer, relay, x_recv, recv):
        for dx in (2, 1, 3):
            block = src_of(peer(dx, wave(k)))
            if wave(k):
                remote(block, relay.at[k, dx - 1], to_x, x_recv.at[k], d, peer(dx, 0)).start()
            else:
                remote(block, buffer(pl.ds(slot_of(z, dx), 1)).at[0], to_x, recv.at[k], d, peer(dx, 0)).start()

    def own_column(k, src_of, buffer, recv):
        there = peer(0, wave(k))
        mine = buffer(pl.ds(slot_of(z, 0), 1)).at[0]
        if wave(k):
            remote(src_of(there), mine, to_z, recv.at[k], d, there).start()

    def relay_column(k, buffer, relay, x_recv, recv):
        if wave(k):
            wait_recv(relay.at[k], x_recv.at[k])
            remote(relay.at[k], buffer(pl.ds(slot_of(z, 1), X - 1)), to_z, recv.at[k], d, peer(0, wave(k))).start()

    def out_src(there):
        return outputs.at[there, d]

    def out_at(slots):
        return outs.at[d, slots]

    def in_src(there):
        return inputs.at[there]

    def in_at(slots):
        return ins.at[slots]

    for k in range(Z):
        own_column(k, out_src, out_at, out_recv)
        to_columns(k, out_src, out_at, relay_outs, x_out_recv, out_recv)
    remote(partials.at[:, 1 - c], rows_core, to_rows, row_recv.at[0], sibling, e).start()

    def rows_of_chip():
        own_rows.wait()
        wait_recv(rows_core, row_recv.at[0])
        rows[...] += rows_core[...]
        remote(rows.at[across], rows_hop.at[0], to_rows, hop_recv.at[0], 2 * ahead + c, e).start()
        remote(rows.at[behind], rows_hop.at[1], to_rows, hop_recv.at[1], 2 * behind + c, e).start()

    def rows_of_two_chips():
        wait_recv(rows_hop.at[0], hop_recv.at[0])
        rows[ahead] += rows_hop[0]
        remote(rows.at[ahead], rows_hop.at[2], to_rows, hop_recv.at[2], 2 * ahead + c, e).start()

    def own(k):
        piece = outs.at[d, slots_from(k)]
        wait_recv(piece, out_recv.at[k])
        remote(piece, piece, to_y, y_recv.at[k, 0], 2 * ahead + c, e).start()
        remote(piece, piece, to_y, y_recv.at[k, 1], 2 * behind + c, e).start()
        remote(piece, piece, to_core, core_recv.at[k, 0], sibling, e).start()

    def near(k):
        piece = outs.at[2 * behind + c, slots_from(k)]
        wait_recv(piece, y_recv.at[k, 0])
        remote(piece, piece, to_y, y_recv.at[k, 2], 2 * ahead + c, e).start()
        remote(piece, piece, to_core, core_recv.at[k, 1], sibling, e).start()
        piece = outs.at[2 * ahead + c, slots_from(k)]
        wait_recv(piece, y_recv.at[k, 1])
        remote(piece, piece, to_core, core_recv.at[k, 2], sibling, e).start()

    def far(k):
        piece = outs.at[2 * across + c, slots_from(k)]
        wait_recv(piece, y_recv.at[k, 2])
        remote(piece, piece, to_core, core_recv.at[k, 3], sibling, e).start()

    def send_tail(k):
        there = peer(0, wave(k))
        recv = tail_recv.at[k - TAIL[0]]
        remote(in_src(there), ins.at[slot_of(z, 0)], to_z, recv.at[0], d, there).start()
        wait_recv(relay_ins.at[k], x_in_recv.at[k])
        for dx in range(1, X):
            remote(relay_ins.at[k, dx - 1], ins.at[slot_of(z, dx)], to_z, recv.at[dx], d, there).start()

    def gathered(k):
        slots = slots_from(k)
        wait_recv(outs.at[sibling, slots], core_recv.at[k, 0])
        wait_recv(outs.at[2 * ahead + 1 - c, slots], core_recv.at[k, 1])
        wait_recv(outs.at[2 * behind + 1 - c, slots], core_recv.at[k, 2])
        wait_recv(outs.at[2 * across + 1 - c, slots], core_recv.at[k, 3])

    def product(pieces):
        left, right = [], []
        for k, dx in pieces:
            from_z = lax.rem(z + Z - wave(k), Z)
            block = ins[slot_of(from_z, dx)]
            slot = BF16_ROWS * lax.broadcasted_iota(jnp.int32, block.shape, 0) + lax.broadcasted_iota(jnp.int32, block.shape, 1)
            count = counts[lax.rem(x + X - dx, X) * Z + from_z, e]
            left.append(jnp.where(slot < count, block, jnp.zeros_like(block)).reshape(-1, block.shape[-1]))
            right.append(outs[:, slot_of(from_z, dx)].reshape(-1, outs.shape[-1]))
        return lax.dot_general(
            jnp.concatenate(left, axis=0),
            jnp.concatenate(right, axis=0),
            (((0,), (0,)), ((), ())),
            preferred_element_type=jnp.float32,
        )

    def multiply(k):
        gathered(k)
        wait_recv(ins.at[slots_from(k)], in_recv.at[k])
        whole = product([(k, dx) for dx in range(X)])
        if k == 0:
            grad[...] = whole
        else:
            grad[...] += whole

    for i in range(Z + 5):
        if i < Z:
            relay_column(i, out_at, relay_outs, x_out_recv, out_recv)
            to_columns(i, in_src, in_at, relay_ins, x_in_recv, in_recv)
        if 3 <= i < Z + 3:
            own(i - 3)
        if 4 <= i < Z + 4:
            if i - 4 in TAIL:
                send_tail(i - 4)
            else:
                own_column(i - 4, in_src, in_at, in_recv)
                relay_column(i - 4, in_at, relay_ins, x_in_recv, in_recv)
            near(i - 4)
        for k in {11: (0, 1), 12: (2, 3)}.get(i, ()):
            multiply(k)
        if 5 <= i:
            far(i - 5)
        if i == 2:
            load_counts.wait()
            rows_of_chip()
        if i == 4:
            rows_of_two_chips()

    wait_recv(rows_hop.at[1], hop_recv.at[1])
    wait_recv(rows_hop.at[2], hop_recv.at[2])
    dense[...] = (rows[y] + rows_hop[1]) + rows_hop[2]

    for k in (4, 7):
        multiply(k)
    for k in TAIL:
        gathered(k)
    for dx in range(X):
        for k in TAIL:
            piece = slot_of(lax.rem(z + Z - wave(k), Z), dx)
            wait_recv(ins.at[piece], tail_recv.at[k - TAIL[0], dx])
        grad[...] += product([(k, dx) for k in TAIL])

    def wait_send(ref, sem):
        remote(ref, ref, sem, sem, d, e).wait_send()

    wait_send(outs.at[0, pl.ds(0, Z * (X - 1))], to_x)
    wait_send(ins.at[pl.ds(0, Z * (X - 1))], to_x)
    wait_send(outs.at[0, pl.ds(0, (Z - 1) * X)], to_z)
    wait_send(ins.at[pl.ds(0, (Z - 1) * X)], to_z)
    wait_send(rows, to_rows)
    wait_send(rows_hop, to_rows)
    wait_send(outs.at[pl.ds(0, 3)], to_y)
    wait_send(outs.at[pl.ds(0, 4)], to_core)


def per_device(
    dense_partials,
    dense_param,
    dense_m,
    dense_v,
    sent_inputs,
    sent_outputs,
    counts,
    expert_param,
    expert_m,
    expert_v,
):
    blocks, slots, width_in = sent_inputs.shape
    width_out = sent_outputs.shape[2]
    part = slots // DP
    dense_rows, dense_width = dense_partials.shape[1] // DP, dense_partials.shape[2]
    dma = pltpu.SemaphoreType.DMA
    expert_grad, dense_grad = pl.pallas_call(
        exchange,
        name="exchange",
        out_shape=(
            jax.ShapeDtypeStruct((width_in, width_out), jnp.float32),
            jax.ShapeDtypeStruct((dense_rows, dense_width), jnp.float32),
        ),
        in_specs=[pl.BlockSpec(memory_space=pltpu.HBM)] * 4,
        out_specs=(pl.BlockSpec(memory_space=pltpu.VMEM),) * 2,
        scratch_shapes=[
            pltpu.SMEM(counts.shape, counts.dtype),
            pltpu.VMEM((blocks, DP, part, width_in), jnp.bfloat16),
            pltpu.VMEM((DP, blocks, part, width_out), jnp.bfloat16),
            pltpu.VMEM((Z - 1, X - 1, DP, part, width_in), jnp.bfloat16),
            pltpu.VMEM((Z - 1, X - 1, part, width_out), jnp.bfloat16),
            pltpu.VMEM((Y, dense_rows, dense_width), jnp.float32),
            pltpu.VMEM((Y, dense_rows, dense_width), jnp.float32),
            pltpu.VMEM((3, dense_rows, dense_width), jnp.float32),
            dma,
            dma((5,)),
            dma((Z - 1,)),
            dma((Z - 1,)),
            dma((Z,)),
            dma((Z,)),
            dma((len(TAIL), X)),
            dma((2,)),
            dma((3,)),
            dma((Z, 3)),
            dma((Z, 4)),
        ],
        cost_estimate=pl.CostEstimate(
            flops=2 * blocks * slots * width_in * width_out,
            bytes_accessed=2 * blocks * slots * (width_in + width_out),
            transcendentals=0,
        ),
        compiler_params=pltpu.CompilerParams(collective_id=0, has_side_effects=True, vmem_limit_bytes=48 << 20),
    )(
        *(
            pltpu.with_memory_space_constraint(operand, pltpu.HBM)
            for operand in (
                counts,
                dense_partials.reshape(Y, 2, dense_rows, dense_width),
                sent_inputs.reshape(blocks, DP, part, width_in),
                sent_outputs.reshape(blocks, DP, part, width_out),
            )
        )
    )
    dense_state = (dense_param, dense_m, dense_v)
    expert_state = tuple(leaf[0] for leaf in (expert_param, expert_m, expert_v))
    dense_new, expert_new = pl.pallas_call(
        update,
        name="update",
        out_shape=tuple(tuple(jax.ShapeDtypeStruct(leaf.shape, leaf.dtype) for leaf in state) for state in (dense_state, expert_state)),
        in_specs=((pl.BlockSpec(memory_space=pltpu.VMEM),) * 4,) * 2,
        out_specs=((pl.BlockSpec(memory_space=pl.ANY),) * 3,) * 2,
        scratch_shapes=[
            tuple(pltpu.VMEM(leaf.shape, leaf.dtype) for leaf in dense_state),
            tuple(pltpu.VMEM(leaf.shape, leaf.dtype) for leaf in expert_state),
            dma((3 * (len(STRETCHES) + 1),)),
        ],
        compiler_params=pltpu.CompilerParams(vmem_limit_bytes=24 << 20),
    )((*dense_state, dense_grad), (*expert_state, expert_grad))
    return (*dense_new, *(leaf[None] for leaf in expert_new))


def solution(mesh):
    in_specs = (
        P("dp", None, "expert"),
        P("dp", "expert"),
        P("dp", "expert"),
        P("dp", "expert"),
        P("expert", None, "dp"),
        P("expert", None, None),
        P(),
        P("expert", "dp", None),
        P("expert", "dp", None),
        P("expert", "dp", None),
    )
    out_specs = (
        P("dp", "expert"),
        P("dp", "expert"),
        P("dp", "expert"),
        P("expert", "dp", None),
        P("expert", "dp", None),
        P("expert", "dp", None),
    )
    return jax.shard_map(per_device, mesh=mesh, in_specs=in_specs, out_specs=out_specs, check_vma=False)
```
